512 devices in a mesh: depth: 8 (over z_lo), row: 8 (over x, core), col: 8 (over z_hi, y).
Axes of the slice: x: 4, y: 4, z: 16 (z_hi: 2, z_lo: 8; z = z_hi * 8 + z_lo), core: 2. Of those that a mesh axis runs over, the one named last changes fastest.
Arguments:
- inputs: bfloat16 [512, 12288], P(('depth', 'row'), 'col'), may hold values from -6 to 6
- pre_act: bfloat16 [512, 24576], P('col', ('depth', 'row')), may hold values from -8 to 8
- out_grad: bfloat16 [512, 12288], P(('depth', 'row'), 'col'), may hold values from -4 to 4
- w_in: bfloat16 [12288, 24576], P('col', ('depth', 'row')), may hold values from -0.0546875 to 0.0546875
- w_out: bfloat16 [24576, 12288], P(('depth', 'row'), 'col'), may hold values from -0.0390625 to 0.0390625
Outputs:
- grad_inputs: bfloat16 [512, 12288], P(('depth', 'row'), 'col')
- grad_w_in: bfloat16 [12288, 24576], P('col', ('depth', 'row'))
- grad_w_out: bfloat16 [24576, 12288], P(('depth', 'row'), 'col')
The draws below stay inside these ranges and needn't reach their ends.
All inputs are finite; a program needn't handle non-finite values.
Results may differ from the reference program's by a relative error of at most 0.0049.
Values may be sent and summed in bfloat16 or wider, within the bound.
No kernel may reach another device: no remote copies, remote signals or barrier semaphores. Data moves between devices by JAX's collectives and lax.ppermute only.
A program may use at most 64 MiB of HBM per device.

```python
import jax
import jax.numpy as jnp

D = 12288
FW = 24576
TOKENS = 512


def block_scale(key, shape, pieces, least, largest):
    def one(dim, parts):
        steps = jax.random.uniform(jax.random.fold_in(jax.random.fold_in(key, 6), dim), (parts,), jnp.float32, least / len(pieces), largest / len(pieces))
        return jnp.repeat(jnp.exp(steps), shape[dim] // parts).reshape((-1,) + (1,) * (len(shape) - dim - 1))

    gain = one(*pieces[0])
    for cut in pieces[1:]:
        gain = gain * one(*cut)
    return gain


def scatter_about(rng, extent, spread, limit, cuts=(), kind=jnp.bfloat16):
    array = jax.random.normal(rng, extent, jnp.float32) * spread
    if len(cuts) > 0:
        array = block_scale(rng, extent, cuts, -0.22, 0.18) * array
    return jnp.clip(array, min=-limit, max=limit).astype(kind)


def setup_inputs(seed: int = 0) -> dict:
    key_list = jax.random.split(jax.random.key(seed), 6)
    return {
        "inputs": scatter_about(key_list[0], (TOKENS, D), 1.0, 6.0, ((0, 64), (1, 8))),
        "pre_act": scatter_about(key_list[1], (TOKENS, FW), 1.5, 8.0, ((0, 8), (1, 64))),
        "out_grad": scatter_about(key_list[2], (TOKENS, D), 0.5, 4.0, ((0, 64), (1, 8))),
        "w_in": scatter_about(key_list[3], (D, FW), D ** -0.5, 0.0546875, ((0, 8), (1, 64))),
        "w_out": scatter_about(key_list[4], (FW, D), FW ** -0.5, 0.0390625, ((0, 64), (1, 8))),
    }


gelu_coeff = 0.7978845608028654
cubic_coeff = 0.044715


def gelu_parts(pre_act):
    pre_float = pre_act.astype(jnp.float32)
    inner_value = gelu_coeff * (pre_float + cubic_coeff * pre_float * pre_float * pre_float)
    tanh_value = jnp.tanh(inner_value)
    activation = 0.5 * pre_float * (1.0 + tanh_value)
    derivative = 0.5 * (1.0 + tanh_value) + 0.5 * pre_float * (1.0 - tanh_value * tanh_value) * gelu_coeff * (1.0 + 3.0 * cubic_coeff * pre_float * pre_float)
    return activation, derivative


def reference(inputs, pre_act, out_grad, w_in, w_out):
    hidden_grad = jnp.dot(out_grad, w_out.T, preferred_element_type=jnp.float32)
    activation, derivative = gelu_parts(pre_act)
    act_bf = activation.astype(jnp.bfloat16)
    delta = (hidden_grad * derivative).astype(jnp.bfloat16)
    grad_w_out = jnp.dot(act_bf.T, out_grad, preferred_element_type=jnp.float32).astype(jnp.bfloat16)
    grad_w_in = jnp.dot(inputs.T, delta, preferred_element_type=jnp.float32).astype(jnp.bfloat16)
    grad_inputs = jnp.dot(delta, w_in.T, preferred_element_type=jnp.float32).astype(jnp.bfloat16)
    return grad_inputs, grad_w_in, grad_w_out
```

```python
import jax
import jax.numpy as jnp
from jax import lax
from jax.sharding import Mesh, PartitionSpec as P

gelu_coeff = 0.7978845608028654
cubic_coeff = 0.044715
bf16 = jnp.bfloat16
f32 = jnp.float32


def gelu_parts(pre_act):
    pre_float = pre_act.astype(jnp.float32)
    inner_value = gelu_coeff * (pre_float + cubic_coeff * pre_float * pre_float * pre_float)
    tanh_value = jnp.tanh(inner_value)
    activation = 0.5 * pre_float * (1.0 + tanh_value)
    derivative = 0.5 * (1.0 + tanh_value) + 0.5 * pre_float * (
        1.0 - tanh_value * tanh_value
    ) * gelu_coeff * (1.0 + 3.0 * cubic_coeff * pre_float * pre_float)
    return (activation, derivative)


def spread(value, axis, size):
    copies = jnp.broadcast_to(value[None], (size,) + value.shape)
    return lax.all_to_all(copies, axis, 0, 0)


def swap(value, axis):
    return lax.ppermute(value, axis, [(0, 1), (1, 0)])


def dot_rows(rows, weights):
    return lax.dot_general(rows, weights, (((1,), (1,)), ((), ())), preferred_element_type=f32)


def dot_tokens(left, right):
    return lax.dot_general(left, right, (((0,), (0,)), ((), ())), preferred_element_type=f32)


def on_device(inputs, pre_act, out_grad, w_in, w_out):
    core = lax.axis_index("c")
    half = lax.axis_index("h")
    D = out_grad.shape[1]
    F = w_out.shape[0]

    both = spread(jnp.stack([out_grad, inputs]), "z", 8)
    grad_z = both[:, 0].reshape(64, D)
    input_z = both[:, 1].reshape(64, D)
    input_rows = lax.all_gather(input_z, ("x", "c"), axis=0, tiled=True)
    grad_own = spread(grad_z, "x", 4).reshape(256, D)
    grad_sib = swap(grad_own, "c")

    part_own = dot_rows(grad_own, w_out).reshape(4, 2, 4, 8, F)
    part_sib = dot_rows(grad_sib, w_out).reshape(4, 2, 4, 8, F)
    parts = jnp.stack([part_own, part_sib], axis=3).transpose(2, 1, 0, 3, 4, 5).astype(bf16)
    parts = lax.all_to_all(parts.reshape(4, 128, F), "y", 0, 0)
    share = jnp.sum(parts.astype(f32), axis=0)

    pre_parts = pre_act.reshape(4, 2, 8, F)
    pre_rel = jnp.where(core == 0, pre_parts, pre_parts[:, ::-1]).reshape(64, F)
    other = swap(jnp.concatenate([share.astype(bf16), pre_rel]), "h")
    hidden_grad = share + other[:128].astype(f32)
    pre_other = other[128:]
    pre_all = jnp.concatenate(
        [jnp.where(half == 0, pre_rel, pre_other), jnp.where(half == 0, pre_other, pre_rel)]
    )
    activation, derivative = gelu_parts(pre_all)
    delta = (hidden_grad * derivative).astype(bf16)
    act = activation.astype(bf16)

    cols = spread(jnp.stack([delta, act]), "y", 4)
    cols = cols.reshape(4, 2, 2, 4, 2, 8, F).transpose(1, 4, 3, 2, 0, 5, 6)
    delta_rel = cols[0].reshape(2, 256, F)
    act_rel = cols[1].reshape(2, 256, F)

    to_sib = dot_rows(delta_rel[1], w_in).astype(bf16)
    from_sib = swap(to_sib, "c")
    own = dot_rows(delta_rel[0], w_in) + from_sib.astype(f32)
    by_x = lax.all_to_all(own.astype(bf16).reshape(4, 64, D), "x", 0, 0)
    own = jnp.sum(by_x.astype(f32), axis=0)
    by_z = lax.all_to_all(own.astype(bf16).reshape(8, 8, D), "z", 0, 0)
    grad_inputs = jnp.sum(by_z.astype(f32), axis=0).astype(bf16)

    grad_w_out = dot_tokens(act_rel[0], grad_own) + dot_tokens(act_rel[1], grad_sib)
    delta_abs = jnp.where(core == 0, delta_rel, delta_rel[::-1])
    delta_abs = delta_abs.reshape(2, 4, 64, F).transpose(1, 0, 2, 3).reshape(512, F)
    grad_w_in = dot_tokens(input_rows, delta_abs)
    return (grad_inputs, grad_w_in.astype(bf16), grad_w_out.astype(bf16))


def solution(mesh):
    fine = Mesh(mesh.devices.reshape(8, 4, 2, 2, 4), ("z", "x", "c", "h", "y"))
    rows, cols = ("z", "x", "c"), ("h", "y")
    in_specs = (P(rows, cols), P(cols, rows), P(rows, cols), P(cols, rows), P(rows, cols))
    out_specs = (P(rows, cols), P(cols, rows), P(rows, cols))
    return jax.shard_map(
        on_device, mesh=fine, in_specs=in_specs, out_specs=out_specs, check_vma=False
    )
```

```python
import jax
import jax.numpy as jnp
from jax import lax
from jax.sharding import Mesh, PartitionSpec as P

gelu_coeff = 0.7978845608028654
cubic_coeff = 0.044715
bf16 = jnp.bfloat16
f32 = jnp.float32


def gelu_parts(pre_act):
    pre_float = pre_act.astype(jnp.float32)
    inner_value = gelu_coeff * (pre_float + cubic_coeff * pre_float * pre_float * pre_float)
    tanh_value = jnp.tanh(inner_value)
    activation = 0.5 * pre_float * (1.0 + tanh_value)
    derivative = 0.5 * (1.0 + tanh_value) + 0.5 * pre_float * (
        1.0 - tanh_value * tanh_value
    ) * gelu_coeff * (1.0 + 3.0 * cubic_coeff * pre_float * pre_float)
    return (activation, derivative)


def spread(value, axis, size):
    copies = jnp.broadcast_to(value[None], (size,) + value.shape)
    return lax.all_to_all(copies, axis, 0, 0)


def swap(value, axis):
    return lax.ppermute(value, axis, [(0, 1), (1, 0)])


def after(value, other):
    return lax.optimization_barrier((value, other))[0]


def turn(value, axis, step):
    size = lax.axis_size(axis)
    return lax.ppermute(value, axis, [((i + step) % size, i) for i in range(size)])


def flip(value, axis, bit):
    size = lax.axis_size(axis)
    return lax.ppermute(value, axis, [(i, i ^ bit) for i in range(size)])


def join(value, other, axis, bit, at):
    upper = (lax.axis_index(axis) & bit) != 0
    return jnp.stack([jnp.where(upper, other, value), jnp.where(upper, value, other)], axis=at)


def dot_rows(rows, weights):
    return lax.dot_general(rows, weights, (((1,), (1,)), ((), ())), preferred_element_type=f32)


def dot_tokens(left, right):
    return lax.dot_general(left, right, (((0,), (0,)), ((), ())), preferred_element_type=f32)


def on_device(inputs, pre_act, out_grad, w_in, w_out):
    core = lax.axis_index("c")
    half = lax.axis_index("h")
    D = out_grad.shape[1]
    F = w_out.shape[0]

    place = lax.axis_index("x")
    copies = jnp.broadcast_to(out_grad[None], (8,) + out_grad.shape)
    grad_z = lax.all_to_all(copies, "z", 0, 0).reshape(64, D)
    other = after(flip(inputs, "z", 4), grad_z)
    block = join(inputs, other, "z", 4, 0)
    pre_parts = pre_act.reshape(4, 2, 8, F)
    pre_parts = jnp.where((place & 1) != 0, pre_parts.reshape(2, 2, 2, 8, F)[:, ::-1].reshape(4, 2, 8, F), pre_parts)
    pre_parts = jnp.where((place & 2) != 0, pre_parts.reshape(2, 2, 2, 8, F)[::-1].reshape(4, 2, 8, F), pre_parts)
    w_out_sib = swap(w_out, "c")
    pre_mine = jnp.where(core == 0, pre_parts[:, 0], pre_parts[:, 1])
    pre_give = jnp.where(core == 0, pre_parts[:, 1], pre_parts[:, 0])
    pre_rel = jnp.stack([pre_mine, swap(pre_give, "c")]).reshape(64, F)
    grad_own = jnp.concatenate([grad_z] + [flip(grad_z, "x", k) for k in (1, 2, 3)])
    other = after(flip(block, "z", 2), grad_own)
    block = join(block, other, "z", 2, 1)
    grad_sib = swap(grad_own, "c")
    w_in_sib = swap(after(w_in, grad_own), "c")
    parts = jnp.stack([dot_rows(grad_own, w_out), dot_rows(grad_own, w_out_sib)])
    parts = parts.reshape(2, 4, 2, 4, 8, F).transpose(3, 0, 2, 1, 4, 5).astype(bf16)
    parts = parts.reshape(4, 128, F)
    summed = lax.all_to_all(parts, "y", 0, 0)
    share = jnp.sum(summed.astype(f32), axis=0)
    other = after(flip(after(block, parts), "z", 1), share)
    block = join(block, other, "z", 1, 2).reshape(64, D)
    other = swap(jnp.concatenate([share.astype(bf16), pre_rel]), "h")
    hidden_grad = share + other[:128].astype(f32)
    pre_other = other[128:]
    pre_rel, pre_other = pre_rel.reshape(2, 1, 32, F), pre_other.reshape(2, 1, 32, F)
    pre_all = jnp.concatenate([jnp.where(half == 0, pre_rel, pre_other), jnp.where(half == 0, pre_other, pre_rel)], axis=1).reshape(128, F)
    activation, derivative = gelu_parts(pre_all)
    delta = (hidden_grad * derivative).astype(bf16)
    act = activation.astype(bf16)
    other = after(flip(after(block, share), "x", 1), delta)
    block = jnp.concatenate([block, other])
    cols = spread(jnp.stack([delta, act]), "y", 4)
    other = after(flip(after(block, delta), "x", 2), cols)
    block = jnp.concatenate([block, other])
    cols = cols.reshape(4, 2, 2, 2, 4, 8, F).transpose(1, 2, 4, 3, 0, 5, 6).reshape(2, 2, 256, F)
    own = dot_rows(cols[0, 0], w_in) + dot_rows(cols[0, 1], w_in_sib)
    far = swap(cols[:, 1].reshape(512, F), "c").reshape(2, 256, F)
    delta_rel = jnp.stack([cols[0, 0], far[0]])
    act_rel = jnp.stack([cols[1, 0], far[1]])
    own = own.reshape(4, 64, D)
    send = own.astype(bf16)
    block_sib = swap(after(block, send), "c")
    own = own[0] + sum(flip(send[k], "x", k).astype(f32) for k in (1, 2, 3))
    by_z = lax.all_to_all(own.astype(bf16).reshape(8, 8, D), "z", 0, 0)
    grad_inputs = jnp.sum(by_z.astype(f32), axis=0).astype(bf16)
    grad_w_out = dot_tokens(act_rel[0], grad_own) + dot_tokens(act_rel[1], grad_sib)
    grad_w_in = dot_tokens(block, delta_rel[0]) + dot_tokens(block_sib, delta_rel[1])
    return (grad_inputs, grad_w_in.astype(bf16), grad_w_out.astype(bf16))

def solution(mesh):
    fine = Mesh(mesh.devices.reshape(8, 4, 2, 2, 4), ("z", "x", "c", "h", "y"))
    rows, cols = ("z", "x", "c"), ("h", "y")
    in_specs = (P(rows, cols), P(cols, rows), P(rows, cols), P(cols, rows), P(rows, cols))
    out_specs = (P(rows, cols), P(cols, rows), P(rows, cols))
    return jax.shard_map(
        on_device, mesh=fine, in_specs=in_specs, out_specs=out_specs, check_vma=False
    )
```

```python
import jax
import jax.numpy as jnp
from jax import lax
from jax.experimental import pallas as pl
from jax.experimental.pallas import tpu as pltpu
from jax.sharding import Mesh, PartitionSpec as P

gelu_coeff = 0.7978845608028654
cubic_coeff = 0.044715
bf16 = jnp.bfloat16
f32 = jnp.float32


def gelu_parts(pre_act):
    pre_float = pre_act.astype(jnp.float32)
    inner_value = gelu_coeff * (pre_float + cubic_coeff * pre_float * pre_float * pre_float)
    tanh_value = jnp.tanh(inner_value)
    activation = 0.5 * pre_float * (1.0 + tanh_value)
    derivative = 0.5 * (1.0 + tanh_value) + 0.5 * pre_float * (
        1.0 - tanh_value * tanh_value
    ) * gelu_coeff * (1.0 + 3.0 * cubic_coeff * pre_float * pre_float)
    return (activation, derivative)


def spread(value, axis, size):
    copies = jnp.broadcast_to(value[None], (size,) + value.shape)
    return lax.all_to_all(copies, axis, 0, 0)


def swap(value, axis):
    return lax.ppermute(value, axis, [(0, 1), (1, 0)])


def after(value, other):
    return lax.optimization_barrier((value, other))[0]


def turn(value, axis, step):
    size = lax.axis_size(axis)
    return lax.ppermute(value, axis, [((i + step) % size, i) for i in range(size)])


def flip(value, axis, bit):
    size = lax.axis_size(axis)
    return lax.ppermute(value, axis, [(i, i ^ bit) for i in range(size)])


def join(value, other, axis, bit, at):
    upper = (lax.axis_index(axis) & bit) != 0
    return jnp.stack([jnp.where(upper, other, value), jnp.where(upper, value, other)], axis=at)


def dot_rows(rows, weights):
    return lax.dot_general(rows, weights, (((1,), (1,)), ((), ())), preferred_element_type=f32)


def dot_tokens(left, right):
    return lax.dot_general(left, right, (((0,), (0,)), ((), ())), preferred_element_type=f32)


def blocks_of_8(value, order):
    return jnp.concatenate([value[8 * k : 8 * k + 8] for k in order])


def call(kernel, out_shape, flops, *operands):
    size = sum(a.size * a.dtype.itemsize for a in (*operands, *out_shape))
    return pl.pallas_call(
        kernel,
        out_shape=out_shape,
        in_specs=[pl.BlockSpec(memory_space=pltpu.VMEM)] * len(operands),
        out_specs=[pl.BlockSpec(memory_space=pltpu.VMEM)] * len(out_shape),
        compiler_params=pltpu.CompilerParams(vmem_limit_bytes=40 * 1024 * 1024),
        cost_estimate=pl.CostEstimate(flops=flops, bytes_accessed=size, transcendentals=0),
    )(*operands)


def hidden_kernel(x0, x1, x2, x3, w_own, w_sib, parts):
    rows = jnp.concatenate([x0[...], x1[...], x2[...], x3[...]])
    for f, w in enumerate((w_own, w_sib)):
        product = dot_rows(rows, w[...])
        for y in range(4):
            order = [x * 8 + h * 4 + y for h in range(2) for x in range(4)]
            parts[y, f * 64 : f * 64 + 64, :] = blocks_of_8(product, order).astype(bf16)


def input_kernel(cols, w_own, w_sib, own, s1, s2, s3, far):
    near_rows = jnp.concatenate([cols[y, 0, 0:64, :] for y in range(4)])
    far_rows = jnp.concatenate([cols[y, 0, 64:128, :] for y in range(4)])
    width = w_own.shape[0]
    step = 512
    for at in range(0, width, step):
        product = dot_rows(near_rows, w_own[at : at + step, :]) + dot_rows(far_rows, w_sib[at : at + step, :])
        for x, out in enumerate((own, s1, s2, s3)):
            order = [y * 8 + h * 4 + x for h in range(2) for y in range(4)]
            out[:, at : at + step] = blocks_of_8(product, order).astype(out.dtype)
    for kind in range(2):
        far[kind] = jnp.concatenate([cols[y, kind, 64:128, :] for y in range(4)])


def by_place(near, far):
    order = [y * 8 + h * 4 + x for x in range(4) for h in range(2) for y in range(4)]
    return [blocks_of_8(v.astype(f32), order).astype(bf16) for v in (near, far)]


def grad_out_kernel(cols, far, grad_own, grad_sib, out):
    near, other = by_place(jnp.concatenate([cols[y, 1, 0:64, :] for y in range(4)]), far[1])
    step = 512
    for at in range(0, grad_own.shape[1], step):
        out[:, at : at + step] = (
            dot_tokens(near, grad_own[:, at : at + step]) + dot_tokens(other, grad_sib[:, at : at + step])
        ).astype(bf16)


def grad_in_kernel(cols, far, block_own, block_sib, out):
    near, other = by_place(jnp.concatenate([cols[y, 0, 0:64, :] for y in range(4)]), far[0])
    step = 256
    for at in range(0, block_own.shape[1], step):
        out[at : at + step, :] = (
            dot_tokens(block_own[:, at : at + step], near) + dot_tokens(block_sib[:, at : at + step], other)
        ).astype(bf16)


def on_device(inputs, pre_act, out_grad, w_in, w_out):
    core = lax.axis_index("c")
    half = lax.axis_index("h")
    D = out_grad.shape[1]
    F = w_out.shape[0]

    place = lax.axis_index("x")
    copies = jnp.broadcast_to(out_grad[None], (8,) + out_grad.shape)
    grad_z = lax.all_to_all(copies, "z", 0, 0).reshape(64, D)
    other = after(flip(inputs, "z", 4), grad_z)
    block = join(inputs, other, "z", 4, 0)
    pre_parts = pre_act.reshape(4, 2, 8, F)
    pre_parts = jnp.where((place & 1) != 0, pre_parts.reshape(2, 2, 2, 8, F)[:, ::-1].reshape(4, 2, 8, F), pre_parts)
    pre_parts = jnp.where((place & 2) != 0, pre_parts.reshape(2, 2, 2, 8, F)[::-1].reshape(4, 2, 8, F), pre_parts)
    w_out_sib = swap(w_out, "c")
    pre_mine = jnp.where(core == 0, pre_parts[:, 0], pre_parts[:, 1])
    pre_give = jnp.where(core == 0, pre_parts[:, 1], pre_parts[:, 0])
    pre_rel = jnp.stack([pre_mine, swap(pre_give, "c")]).reshape(64, F)
    grad_x = [grad_z] + [flip(grad_z, "x", k) for k in (1, 2, 3)]
    other = after(flip(block, "z", 2), grad_x[3])
    block = join(block, other, "z", 2, 1)
    (parts,) = call(
        hidden_kernel, [jax.ShapeDtypeStruct((4, 128, F), bf16)], 2 * 512 * D * F, *grad_x, w_out, w_out_sib
    )
    summed = lax.all_to_all(parts, "y", 0, 0)
    share = jnp.sum(summed.astype(f32), axis=0)
    other = after(flip(after(block, parts), "z", 1), share)
    w_in_sib = after(swap(after(w_in, parts), "c"), share)
    block = join(block, other, "z", 1, 2).reshape(64, D)
    other = swap(jnp.concatenate([share.astype(bf16), pre_rel]), "h")
    hidden_grad = share + other[:128].astype(f32)
    pre_other = other[128:]
    pre_rel, pre_other = pre_rel.reshape(2, 1, 32, F), pre_other.reshape(2, 1, 32, F)
    pre_all = jnp.concatenate([jnp.where(half == 0, pre_rel, pre_other), jnp.where(half == 0, pre_other, pre_rel)], axis=1).reshape(128, F)
    activation, derivative = gelu_parts(pre_all)
    delta = (hidden_grad * derivative).astype(bf16)
    act = activation.astype(bf16)
    other = flip(after(block, share), "x", 1)
    delta, act, other = lax.optimization_barrier((delta, act, other))
    block = jnp.concatenate([block, other])
    grad_own = jnp.concatenate(grad_x)
    grad_sib = swap(after(grad_own, delta), "c")
    cols = spread(jnp.stack([delta, act]), "y", 4)
    other = flip(after(block, delta), "x", 2)
    cols = cols.reshape(4, 2, 128, F)
    piece = jax.ShapeDtypeStruct((64, D), bf16)
    own, send_1, send_2, send_3, far = call(
        input_kernel,
        [jax.ShapeDtypeStruct((64, D), f32), piece, piece, piece, jax.ShapeDtypeStruct((2, 256, F), bf16)],
        2 * 512 * D * F,
        cols,
        w_in,
        w_in_sib,
    )
    other = after(other, own)
    block = jnp.concatenate([block, other])
    far = swap(far, "c")
    sums = [flip(v, "x", k).astype(f32) for k, v in ((1, send_1), (2, send_2), (3, send_3))]
    own, far = lax.optimization_barrier((own + sums[0] + sums[1] + sums[2], far))
    block_sib = swap(after(block, own), "c")
    by_z = lax.all_to_all(own.astype(bf16).reshape(8, 8, D), "z", 0, 0)
    (grad_w_out,) = call(
        grad_out_kernel, [jax.ShapeDtypeStruct((F, D), bf16)], 2 * 512 * D * F, cols, far, grad_own, grad_sib
    )
    (grad_w_in,) = call(
        grad_in_kernel, [jax.ShapeDtypeStruct((D, F), bf16)], 2 * 512 * D * F, cols, far, block, block_sib
    )
    by_z = after(by_z, grad_w_in)
    grad_inputs = jnp.sum(by_z.astype(f32), axis=0).astype(bf16)
    return (grad_inputs, grad_w_in, grad_w_out)


def solution(mesh):
    fine = Mesh(mesh.devices.reshape(8, 4, 2, 2, 4), ("z", "x", "c", "h", "y"))
    rows, cols = ("z", "x", "c"), ("h", "y")
    in_specs = (P(rows, cols), P(cols, rows), P(rows, cols), P(cols, rows), P(rows, cols))
    out_specs = (P(rows, cols), P(cols, rows), P(rows, cols))
    return jax.shard_map(
        on_device, mesh=fine, in_specs=in_specs, out_specs=out_specs, check_vma=False
    )
```

```python
import jax
import jax.numpy as jnp
from jax import lax
from jax.experimental import pallas as pl
from jax.experimental.pallas import tpu as pltpu
from jax.sharding import Mesh, PartitionSpec as P

gelu_coeff = 0.7978845608028654
cubic_coeff = 0.044715
bf16 = jnp.bfloat16
f32 = jnp.float32


def gelu_parts(pre_act):
    pre_float = pre_act.astype(jnp.float32)
    inner_value = gelu_coeff * (pre_float + cubic_coeff * pre_float * pre_float * pre_float)
    tanh_value = jnp.tanh(inner_value)
    activation = 0.5 * pre_float * (1.0 + tanh_value)
    derivative = 0.5 * (1.0 + tanh_value) + 0.5 * pre_float * (
        1.0 - tanh_value * tanh_value
    ) * gelu_coeff * (1.0 + 3.0 * cubic_coeff * pre_float * pre_float)
    return (activation, derivative)


def spread(value, axis, size):
    copies = jnp.broadcast_to(value[None], (size,) + value.shape)
    return lax.all_to_all(copies, axis, 0, 0)


def swap(value, axis):
    return lax.ppermute(value, axis, [(0, 1), (1, 0)])


def after(value, other):
    return lax.optimization_barrier((value, other))[0]


def turn(value, axis, step):
    size = lax.axis_size(axis)
    return lax.ppermute(value, axis, [((i + step) % size, i) for i in range(size)])


def flip(value, axis, bit):
    size = lax.axis_size(axis)
    return lax.ppermute(value, axis, [(i, i ^ bit) for i in range(size)])


def join(value, other, axis, bit, at):
    upper = (lax.axis_index(axis) & bit) != 0
    return jnp.stack([jnp.where(upper, other, value), jnp.where(upper, value, other)], axis=at)


def dot_rows(rows, weights):
    return lax.dot_general(rows, weights, (((1,), (1,)), ((), ())), preferred_element_type=f32)


def dot_tokens(left, right):
    return lax.dot_general(left, right, (((0,), (0,)), ((), ())), preferred_element_type=f32)


def blocks_of_8(value, order):
    return jnp.concatenate([value[8 * k : 8 * k + 8] for k in order])


def call(kernel, out_shape, flops, *operands):
    size = sum(a.size * a.dtype.itemsize for a in (*operands, *out_shape))
    return pl.pallas_call(
        kernel,
        out_shape=out_shape,
        in_specs=[pl.BlockSpec(memory_space=pltpu.VMEM)] * len(operands),
        out_specs=[pl.BlockSpec(memory_space=pltpu.VMEM)] * len(out_shape),
        compiler_params=pltpu.CompilerParams(vmem_limit_bytes=16 * 1024 * 1024),
        cost_estimate=pl.CostEstimate(flops=flops, bytes_accessed=size, transcendentals=0),
    )(*operands)


def hidden_kernel(x0, x1, x2, x3, w_own, w_sib, parts):
    rows = jnp.concatenate([x0[...], x1[...], x2[...], x3[...]])
    for f, w in enumerate((w_own, w_sib)):
        product = dot_rows(rows, w[...])
        for y in range(4):
            order = [x * 8 + h * 4 + y for h in range(2) for x in range(4)]
            parts[y, f * 64 : f * 64 + 64, :] = blocks_of_8(product, order).astype(bf16)


def input_kernel(cols, w_own, w_sib, own, s1, s2, s3, far):
    near_rows = jnp.concatenate([cols[y, 0, 0:64, :] for y in range(4)])
    far_rows = jnp.concatenate([cols[y, 0, 64:128, :] for y in range(4)])
    width = w_own.shape[0]
    step = 512
    for at in range(0, width, step):
        product = dot_rows(near_rows, w_own[at : at + step, :]) + dot_rows(far_rows, w_sib[at : at + step, :])
        for x, out in enumerate((own, s1, s2, s3)):
            order = [y * 8 + h * 4 + x for h in range(2) for y in range(4)]
            out[:, at : at + step] = blocks_of_8(product, order).astype(out.dtype)
    for kind in range(2):
        far[kind] = jnp.concatenate([cols[y, kind, 64:128, :] for y in range(4)])


def by_place(near, far):
    order = [y * 8 + h * 4 + x for x in range(4) for h in range(2) for y in range(4)]
    return [blocks_of_8(v.astype(f32), order).astype(bf16) for v in (near, far)]


def grad_out_kernel(cols, far, grad_own, grad_sib, out):
    near, other = by_place(jnp.concatenate([cols[y, 1, 0:64, :] for y in range(4)]), far[1])
    step = 512
    for at in range(0, grad_own.shape[1], step):
        out[:, at : at + step] = (
            dot_tokens(near, grad_own[:, at : at + step]) + dot_tokens(other, grad_sib[:, at : at + step])
        ).astype(bf16)


def grad_in_kernel(cols, far, block_own, block_sib, out):
    near, other = by_place(jnp.concatenate([cols[y, 0, 0:64, :] for y in range(4)]), far[0])
    step = 256
    for at in range(0, block_own.shape[1], step):
        out[at : at + step, :] = (
            dot_tokens(block_own[:, at : at + step], near) + dot_tokens(block_sib[:, at : at + step], other)
        ).astype(bf16)


def on_device(inputs, pre_act, out_grad, w_in, w_out):
    core = lax.axis_index("c")
    half = lax.axis_index("h")
    D = out_grad.shape[1]
    F = w_out.shape[0]

    place = lax.axis_index("x")
    copies = jnp.broadcast_to(out_grad[None], (8,) + out_grad.shape)
    grad_z = lax.all_to_all(copies, "z", 0, 0).reshape(64, D)
    other = after(flip(inputs, "z", 4), grad_z)
    block = join(inputs, other, "z", 4, 0)
    pre_parts = pre_act.reshape(4, 2, 8, F)
    pre_parts = jnp.where((place & 1) != 0, pre_parts.reshape(2, 2, 2, 8, F)[:, ::-1].reshape(4, 2, 8, F), pre_parts)
    pre_parts = jnp.where((place & 2) != 0, pre_parts.reshape(2, 2, 2, 8, F)[::-1].reshape(4, 2, 8, F), pre_parts)
    w_out_sib = swap(w_out, "c")
    pre_mine = jnp.where(core == 0, pre_parts[:, 0], pre_parts[:, 1])
    pre_give = jnp.where(core == 0, pre_parts[:, 1], pre_parts[:, 0])
    pre_rel = jnp.stack([pre_mine, swap(pre_give, "c")]).reshape(64, F)
    grad_x = [grad_z] + [flip(grad_z, "x", k) for k in (1, 2, 3)]
    other = after(flip(block, "z", 2), grad_x[3])
    block = join(block, other, "z", 2, 1)
    (parts,) = call(
        hidden_kernel, [jax.ShapeDtypeStruct((4, 128, F), bf16)], 2 * 512 * D * F, *grad_x, w_out, w_out_sib
    )
    summed = lax.all_to_all(parts, "y", 0, 0)
    share = jnp.sum(summed.astype(f32), axis=0)
    other = after(flip(after(block, parts), "z", 1), share)
    w_in_sib = after(swap(after(w_in, parts), "c"), share)
    block = join(block, other, "z", 1, 2).reshape(64, D)
    other = swap(jnp.concatenate([share.astype(bf16), pre_rel]), "h")
    hidden_grad = share + other[:128].astype(f32)
    pre_other = other[128:]
    pre_rel, pre_other = pre_rel.reshape(2, 1, 32, F), pre_other.reshape(2, 1, 32, F)
    pre_all = jnp.concatenate([jnp.where(half == 0, pre_rel, pre_other), jnp.where(half == 0, pre_other, pre_rel)], axis=1).reshape(128, F)
    activation, derivative = gelu_parts(pre_all)
    delta = (hidden_grad * derivative).astype(bf16)
    act = activation.astype(bf16)
    other = flip(after(block, share), "x", 1)
    delta, act, other = lax.optimization_barrier((delta, act, other))
    block = jnp.concatenate([block, other])
    grad_own = jnp.concatenate(grad_x)
    grad_sib = swap(after(grad_own, delta), "c")
    cols = spread(jnp.stack([delta, act]), "y", 4)
    other = flip(after(block, delta), "x", 2)
    cols = cols.reshape(4, 2, 128, F)
    piece = jax.ShapeDtypeStruct((64, D), bf16)
    own, send_1, send_2, send_3, far = call(
        input_kernel,
        [jax.ShapeDtypeStruct((64, D), f32), piece, piece, piece, jax.ShapeDtypeStruct((2, 256, F), bf16)],
        2 * 512 * D * F,
        cols,
        w_in,
        w_in_sib,
    )
    other = after(other, own)
    block = jnp.concatenate([block, other])
    far = swap(far, "c")
    sums = [flip(v, "x", k).astype(f32) for k, v in ((1, send_1), (2, send_2), (3, send_3))]
    own, far = lax.optimization_barrier((own + sums[0] + sums[1] + sums[2], far))
    block_sib = swap(block, "c")
    by_z = lax.all_to_all(own.astype(bf16).reshape(8, 8, D), "z", 0, 0)
    (grad_w_out,) = call(
        grad_out_kernel, [jax.ShapeDtypeStruct((F, D), bf16)], 2 * 512 * D * F, cols, far, grad_own, grad_sib
    )
    (grad_w_in,) = call(
        grad_in_kernel, [jax.ShapeDtypeStruct((D, F), bf16)], 2 * 512 * D * F, cols, far, block, block_sib
    )
    by_z = after(by_z, grad_w_in)
    grad_inputs = jnp.sum(by_z.astype(f32), axis=0).astype(bf16)
    return (grad_inputs, grad_w_in, grad_w_out)


def solution(mesh):
    fine = Mesh(mesh.devices.reshape(8, 4, 2, 2, 4), ("z", "x", "c", "h", "y"))
    rows, cols = ("z", "x", "c"), ("h", "y")
    in_specs = (P(rows, cols), P(cols, rows), P(rows, cols), P(cols, rows), P(rows, cols))
    out_specs = (P(rows, cols), P(cols, rows), P(rows, cols))
    return jax.shard_map(
        on_device, mesh=fine, in_specs=in_specs, out_specs=out_specs, check_vma=False
    )
```

```python
import jax
import jax.numpy as jnp
from jax import lax
from jax.experimental import pallas as pl
from jax.experimental.pallas import tpu as pltpu
from jax.sharding import Mesh, PartitionSpec as P

gelu_coeff = 0.7978845608028654
cubic_coeff = 0.044715
bf16 = jnp.bfloat16
f32 = jnp.float32


def gelu_parts(pre_act):
    pre_float = pre_act.astype(jnp.float32)
    inner_value = gelu_coeff * (pre_float + cubic_coeff * pre_float * pre_float * pre_float)
    tanh_value = jnp.tanh(inner_value)
    activation = 0.5 * pre_float * (1.0 + tanh_value)
    derivative = 0.5 * (1.0 + tanh_value) + 0.5 * pre_float * (
        1.0 - tanh_value * tanh_value
    ) * gelu_coeff * (1.0 + 3.0 * cubic_coeff * pre_float * pre_float)
    return (activation, derivative)


def spread(value, axis, size):
    copies = jnp.broadcast_to(value[None], (size,) + value.shape)
    return lax.all_to_all(copies, axis, 0, 0)


def swap(value, axis):
    return lax.ppermute(value, axis, [(0, 1), (1, 0)])


def after(value, other):
    return lax.optimization_barrier((value, other))[0]


def turn(value, axis, step):
    size = lax.axis_size(axis)
    return lax.ppermute(value, axis, [((i + step) % size, i) for i in range(size)])


def flip(value, axis, bit):
    size = lax.axis_size(axis)
    return lax.ppermute(value, axis, [(i, i ^ bit) for i in range(size)])


def join(value, other, axis, bit, at):
    upper = (lax.axis_index(axis) & bit) != 0
    return jnp.stack([jnp.where(upper, other, value), jnp.where(upper, value, other)], axis=at)


def dot_rows(rows, weights):
    return lax.dot_general(rows, weights, (((1,), (1,)), ((), ())), preferred_element_type=f32)


def dot_tokens(left, right):
    return lax.dot_general(left, right, (((0,), (0,)), ((), ())), preferred_element_type=f32)


def blocks_of_8(value, order):
    return jnp.concatenate([value[8 * k : 8 * k + 8] for k in order])


def call(kernel, out_shape, flops, *operands):
    size = sum(a.size * a.dtype.itemsize for a in (*operands, *out_shape))
    return pl.pallas_call(
        kernel,
        out_shape=out_shape,
        in_specs=[pl.BlockSpec(memory_space=pltpu.VMEM)] * len(operands),
        out_specs=[pl.BlockSpec(memory_space=pltpu.VMEM)] * len(out_shape),
        compiler_params=pltpu.CompilerParams(vmem_limit_bytes=16 * 1024 * 1024),
        cost_estimate=pl.CostEstimate(flops=flops, bytes_accessed=size, transcendentals=0),
    )(*operands)


def hidden_kernel(x0, x1, x2, x3, w_own, w_sib, parts):
    rows = jnp.concatenate([x0[...], x1[...], x2[...], x3[...]])
    for f, w in enumerate((w_own, w_sib)):
        product = dot_rows(rows, w[...])
        for y in range(4):
            order = [x * 8 + h * 4 + y for h in range(2) for x in range(4)]
            parts[y, f * 64 : f * 64 + 64, :] = blocks_of_8(product, order).astype(bf16)


def input_kernel(cols, w_own, w_sib, own, s1, s2, s3, far):
    near_rows = jnp.concatenate([cols[y, 0, 0:64, :] for y in range(4)])
    far_rows = jnp.concatenate([cols[y, 0, 64:128, :] for y in range(4)])
    width = w_own.shape[0]
    step = 512
    for at in range(0, width, step):
        product = dot_rows(near_rows, w_own[at : at + step, :]) + dot_rows(far_rows, w_sib[at : at + step, :])
        for x, out in enumerate((own, s1, s2, s3)):
            order = [y * 8 + h * 4 + x for h in range(2) for y in range(4)]
            out[:, at : at + step] = blocks_of_8(product, order).astype(out.dtype)
    for kind in range(2):
        far[kind] = jnp.concatenate([cols[y, kind, 64:128, :] for y in range(4)])


def by_place(near, far):
    order = [y * 8 + h * 4 + x for x in range(4) for h in range(2) for y in range(4)]
    return [blocks_of_8(v.astype(f32), order).astype(bf16) for v in (near, far)]


def grad_out_kernel(cols, far, grad_own, grad_sib, out):
    near, other = by_place(jnp.concatenate([cols[y, 1, 0:64, :] for y in range(4)]), far[1])
    step = 512
    for at in range(0, grad_own.shape[1], step):
        out[:, at : at + step] = (
            dot_tokens(near, grad_own[:, at : at + step]) + dot_tokens(other, grad_sib[:, at : at + step])
        ).astype(bf16)


def grad_in_kernel(cols, far, block_own, block_sib, out):
    near, other = by_place(jnp.concatenate([cols[y, 0, 0:64, :] for y in range(4)]), far[0])
    step = 256
    for at in range(0, block_own.shape[1], step):
        out[at : at + step, :] = (
            dot_tokens(block_own[:, at : at + step], near) + dot_tokens(block_sib[:, at : at + step], other)
        ).astype(bf16)


def on_device(inputs, pre_act, out_grad, w_in, w_out):
    core = lax.axis_index("c")
    half = lax.axis_index("h")
    D = out_grad.shape[1]
    F = w_out.shape[0]

    place = lax.axis_index("x")
    copies = jnp.broadcast_to(out_grad[None], (8,) + out_grad.shape)
    grad_z = lax.all_to_all(copies, "z", 0, 0).reshape(64, D)
    other = after(flip(inputs, "z", 4), grad_z)
    block = join(inputs, other, "z", 4, 0)
    pre_parts = pre_act.reshape(4, 2, 8, F)
    pre_parts = jnp.stack(
        [
            jnp.where(
                place < 2,
                jnp.where(place == 0, pre_parts[k], pre_parts[k ^ 1]),
                jnp.where(place == 2, pre_parts[k ^ 2], pre_parts[k ^ 3]),
            )
            for k in range(4)
        ]
    )
    w_out_sib = swap(w_out, "c")
    pre_mine = jnp.where(core == 0, pre_parts[:, 0], pre_parts[:, 1])
    pre_give = jnp.where(core == 0, pre_parts[:, 1], pre_parts[:, 0])
    pre_rel = jnp.stack([pre_mine, swap(pre_give, "c")]).reshape(64, F)
    grad_x = [grad_z] + [flip(grad_z, "x", k) for k in (1, 2, 3)]
    other = after(flip(block, "z", 2), grad_x[3])
    block = join(block, other, "z", 2, 1)
    (parts,) = call(
        hidden_kernel, [jax.ShapeDtypeStruct((4, 128, F), bf16)], 2 * 512 * D * F, *grad_x, w_out, w_out_sib
    )
    summed = lax.all_to_all(parts, "y", 0, 0)
    share = jnp.sum(summed.astype(f32), axis=0)
    other = after(flip(after(block, parts), "z", 1), share)
    w_in_sib = after(swap(after(w_in, parts), "c"), share)
    block = join(block, other, "z", 1, 2).reshape(64, D)
    other = swap(jnp.concatenate([share.astype(bf16), pre_rel]), "h")
    hidden_grad = share + other[:128].astype(f32)
    pre_other = other[128:]
    pre_rel, pre_other = pre_rel.reshape(2, 1, 32, F), pre_other.reshape(2, 1, 32, F)
    pre_all = jnp.concatenate([jnp.where(half == 0, pre_rel, pre_other), jnp.where(half == 0, pre_other, pre_rel)], axis=1).reshape(128, F)
    activation, derivative = gelu_parts(pre_all)
    delta = (hidden_grad * derivative).astype(bf16)
    act = activation.astype(bf16)
    other = flip(after(block, share), "x", 1)
    delta, act, other = lax.optimization_barrier((delta, act, other))
    block = jnp.concatenate([block, other])
    grad_own = jnp.concatenate(grad_x)
    grad_sib = swap(after(grad_own, delta), "c")
    cols = spread(jnp.stack([delta, act]), "y", 4)
    other = flip(after(block, delta), "x", 2)
    cols = cols.reshape(4, 2, 128, F)
    piece = jax.ShapeDtypeStruct((64, D), bf16)
    own, send_1, send_2, send_3, far = call(
        input_kernel,
        [jax.ShapeDtypeStruct((64, D), f32), piece, piece, piece, jax.ShapeDtypeStruct((2, 256, F), bf16)],
        2 * 512 * D * F,
        cols,
        w_in,
        w_in_sib,
    )
    other = after(other, own)
    block = jnp.concatenate([block, other])
    far = swap(far, "c")
    sums = [flip(v, "x", k).astype(f32) for k, v in ((1, send_1), (2, send_2), (3, send_3))]
    own, far = lax.optimization_barrier((own + sums[0] + sums[1] + sums[2], far))
    block_sib = swap(block, "c")
    by_z = lax.all_to_all(own.astype(bf16).reshape(8, 8, D), "z", 0, 0)
    (grad_w_out,) = call(
        grad_out_kernel, [jax.ShapeDtypeStruct((F, D), bf16)], 2 * 512 * D * F, cols, far, grad_own, grad_sib
    )
    (grad_w_in,) = call(
        grad_in_kernel, [jax.ShapeDtypeStruct((D, F), bf16)], 2 * 512 * D * F, cols, far, block, block_sib
    )
    by_z = after(by_z, grad_w_in)
    grad_inputs = jnp.sum(by_z.astype(f32), axis=0).astype(bf16)
    return (grad_inputs, grad_w_in, grad_w_out)


def solution(mesh):
    fine = Mesh(mesh.devices.reshape(8, 4, 2, 2, 4), ("z", "x", "c", "h", "y"))
    rows, cols = ("z", "x", "c"), ("h", "y")
    in_specs = (P(rows, cols), P(cols, rows), P(rows, cols), P(cols, rows), P(rows, cols))
    out_specs = (P(rows, cols), P(cols, rows), P(rows, cols))
    return jax.shard_map(
        on_device, mesh=fine, in_specs=in_specs, out_specs=out_specs, check_vma=False
    )
```
